512 devices in a mesh: fsdp: 64 (over x_hi, z, core), tp: 8 (over y, x_lo).
Axes of the slice: x: 4 (x_hi: 2, x_lo: 2; x = x_hi * 2 + x_lo), y: 4, z: 16, core: 2. Of those that a mesh axis runs over, the one named last changes fastest.
Arguments:
- momentum: float32 [12288, 12288], P('fsdp', 'tp'), may hold values from -96 to 96
- gradient: bfloat16 [12288, 12288], P('fsdp', 'tp'), may hold values from -96 to 96
- q_factor: float32 [8, 1536, 512], P('tp', 'fsdp'), may hold values from -0.0546875 to 0.0546875
Outputs:
- new_momentum: float32 [12288, 12288], P('fsdp', 'tp')
- new_q: float32 [8, 1536, 512], P('tp', 'fsdp')
- update: bfloat16 [12288, 12288], P('fsdp', 'tp')
The draws below stay inside these ranges and needn't reach their ends.
All inputs are finite; a program needn't handle non-finite values.
Results may differ from the reference program's by a relative error of at most 0.001.
Values sent between devices are 32-bit elements; how exact they have to be, the bound alone decides.
No kernel may reach another device: no remote copies, remote signals or barrier semaphores. Data moves between devices by JAX's collectives and lax.ppermute only.
A program may use at most 64 MiB of HBM per device.

```python
import math
import jax
import jax.numpy as jnp
from jax import lax

D_ROWS = 12288
D_COLS = 12288
RANK = 512
N_TP = 8


def common_scales(key):
    row_key = jax.random.fold_in(key, 101)
    col_key = jax.random.fold_in(key, 202)
    row_scale = jnp.exp(jax.random.uniform(row_key, (D_ROWS,), jnp.float32, 0.0, math.log(10.0)))
    col_scale = jnp.exp(jax.random.uniform(col_key, (D_COLS,), jnp.float32, 0.0, math.log(10.0)))
    row_trend = jnp.sqrt(3.0) ** (jnp.arange(D_ROWS, dtype=jnp.float32) / D_ROWS)
    col_trend = jnp.sqrt(3.0) ** (jnp.arange(D_COLS, dtype=jnp.float32) / D_COLS)
    return (row_scale * row_trend / 4.6, col_scale * col_trend / 4.6)


def draw_momentum(key, part):
    base = key
    key = jax.random.fold_in(base, 3)
    row_scale, col_scale = common_scales(base)
    noise = jnp.clip(jax.random.normal(key, (D_ROWS, D_COLS), jnp.float32), -6.0, 6.0)
    return jnp.clip(noise * row_scale[:, None] * col_scale[None, :], -96.0, 96.0).astype(jnp.float32)


def draw_gradient(key, part):
    base = key
    key = jax.random.fold_in(base, 5)
    row_scale, col_scale = common_scales(base)
    noise = jnp.clip(jax.random.normal(key, (D_ROWS, D_COLS), jnp.float32), -6.0, 6.0)
    return jnp.clip(noise * row_scale[:, None] * col_scale[None, :], -96.0, 96.0).astype(jnp.bfloat16)


def shard_levels(key, shape, shards, low, largest):
    factor_of, own = 1.0, jax.random.fold_in(key, 6)
    for axis_at, blocks in shards:
        draws = jnp.exp(jax.random.uniform(jax.random.fold_in(own, axis_at), (blocks,), jnp.float32, low / len(shards), largest / len(shards)))
        factor_of = factor_of * jnp.repeat(draws, shape[axis_at] // blocks).reshape([-1 if axis == axis_at else 1 for axis in range(len(shape))])
    return factor_of


def gaussian(stream_key, dims, width, reach, pieces=(), held_as=jnp.bfloat16):
    drawn = width * jax.random.normal(stream_key, dims, jnp.float32)
    if pieces:
        drawn = drawn * shard_levels(stream_key, dims, pieces, -0.22, 0.18)
    return jnp.clip(drawn, -reach, reach).astype(held_as)


def setup_inputs(seed: int = 0) -> dict:
    splits = jax.random.split(jax.random.key(seed), 4)
    momentum = draw_momentum(jax.random.fold_in(splits[3], 71), 0)
    gradient = draw_gradient(jax.random.fold_in(splits[3], 71), 0)
    q_factor = gaussian(splits[2], (N_TP, D_COLS // N_TP, RANK), D_COLS ** -0.5, 0.0546875, ((0, 8), (1, 64)), jnp.float32)
    return dict(momentum=momentum, gradient=gradient, q_factor=q_factor)


EPSILON = 1e-06
FEEDBACK = 0.1

def column_unit(matrix):
    return matrix / jnp.sqrt(lax.optimization_barrier(jnp.sum(matrix * matrix, axis=0)) + EPSILON)

def reference(momentum, gradient, q_factor):
    precise = lax.Precision.HIGHEST
    blended = momentum + gradient.astype(jnp.float32)
    basis = q_factor.reshape(D_COLS, RANK)
    left = jnp.dot(blended, basis, precision=precise, preferred_element_type=jnp.float32)
    left_unit = column_unit(left)
    right = lax.dot_general(blended, left_unit, (((0,), (0,)), ((), ())), precision=precise, preferred_element_type=jnp.float32)
    basis_next = column_unit(right)
    new_momentum = blended - FEEDBACK * jnp.dot(left_unit, right.T, precision=precise, preferred_element_type=jnp.float32)
    factor = math.sqrt(D_ROWS * D_COLS / RANK)
    update = (factor * jnp.dot(left_unit, basis_next.T, precision=precise, preferred_element_type=jnp.float32)).astype(jnp.bfloat16)
    return (new_momentum, basis_next.reshape(N_TP, D_COLS // N_TP, RANK), update)
```

```python
import math

import jax
import jax.numpy as jnp
from jax import lax
from jax.sharding import Mesh, PartitionSpec as P

D_ROWS = 12288
D_COLS = 12288
RANK = 512
HALF = RANK // 2

EPSILON = 1e-06
FEEDBACK = 0.1

XH, ZH, ZL, CORE = 2, 4, 4, 2
ROW_AXES = ("xh", "zh", "zl", "core")
COL_AXES = ("y", "xl")
N_TP = 8
SHARD = 48
PAIR = [(0, 1), (1, 0)]


def dot(a, b, contract):
    return lax.dot_general(
        a, b, (contract, ((), ())), precision=lax.Precision.HIGH, preferred_element_type=jnp.float32
    )


def exchange(parts, axis):
    return lax.all_to_all(parts, axis, split_axis=0, concat_axis=0, tiled=True)


def spread(block, axis, count):
    return exchange(jnp.broadcast_to(block[None], (count,) + block.shape), axis)


def swap(block, axis):
    return lax.ppermute(block, axis, PAIR)


def gather_half(shard):
    by_zh = spread(shard, "zh", ZH)
    by_zl = spread(by_zh, "zl", ZL)
    return by_zl.transpose(1, 0, 2, 3).reshape(ZH * ZL * SHARD, shard.shape[-1])


def ordered(mine, other, first):
    return jnp.where(first, jnp.concatenate([mine, other]), jnp.concatenate([other, mine]))


def on_device(momentum, gradient, q_factor):
    xh = lax.axis_index("xh")
    core = lax.axis_index("core")
    blended = momentum + gradient.astype(jnp.float32)
    rows, cols = blended.shape
    blended_other = swap(blended, "core")
    pair_rows = jnp.concatenate([blended, blended_other])
    half_cols = cols // XH
    mine_cols = lax.dynamic_slice_in_dim(pair_rows, xh * half_cols, half_cols, 1)
    other_cols = lax.dynamic_slice_in_dim(pair_rows, (1 - xh) * half_cols, half_cols, 1)

    own_q = q_factor[0].reshape(-1, CORE, HALF).transpose(1, 0, 2)
    chip_q = exchange(own_q, "core").reshape(SHARD, HALF)
    basis_mine = gather_half(chip_q)
    basis_other = swap(basis_mine, "xh")

    left_part = dot(mine_cols, basis_mine, ((1,), (0,))) + dot(other_cols, basis_other, ((1,), (0,)))
    by_tp = exchange(left_part.reshape(N_TP, SHARD, HALF), COL_AXES)
    left_own = jnp.sum(by_tp, axis=0)
    left = spread(left_own, COL_AXES, N_TP).reshape(2 * rows, HALF)

    squares = jnp.sum((left * left).reshape(-1, 8, HALF), axis=0)
    send = dot(other_cols, left, ((0,), (0,)))
    got = swap(jnp.concatenate([send, squares]), "xh")
    right = dot(mine_cols, left, ((0,), (0,))) + got[:half_cols]
    squares = squares + got[half_cols:]
    right = right.reshape(ZH, ZL, SHARD, HALF).transpose(1, 0, 2, 3).reshape(ZL, ZH * SHARD, HALF)
    right = jnp.concatenate([right, jnp.broadcast_to(squares[None], (ZL,) + squares.shape)], axis=1)
    right = jnp.sum(exchange(right, "zl"), axis=0)
    squares = right[ZH * SHARD :]
    right = right[: ZH * SHARD].reshape(ZH, SHARD, HALF)
    right = jnp.concatenate([right, jnp.broadcast_to(squares[None], (ZH,) + squares.shape)], axis=1)
    right = jnp.sum(exchange(right, "zh"), axis=0)
    left_norm = jnp.sqrt(jnp.sum(right[SHARD:], axis=0) + EPSILON)
    right = right[:SHARD] / left_norm
    left_unit = left / left_norm
    unit_own = jnp.concatenate([left_unit[:rows], swap(left_unit[rows:], "core")], axis=1)

    right_mine = gather_half(right)
    right_other = swap(right_mine, "xh")
    right_half = ordered(right_mine, right_other, xh == 0)
    right_full = jnp.concatenate([right_half, swap(right_half, "core")], axis=1)

    right_squares = jnp.sum((right_full * right_full).reshape(-1, 8, RANK), axis=0)
    right_squares = jnp.sum(spread(right_squares, COL_AXES, N_TP), axis=(0, 1))
    inverse = 1.0 / jnp.sqrt(right_squares + EPSILON)

    new_momentum = blended - FEEDBACK * dot(unit_own, right_full, ((1,), (1,)))
    factor = math.sqrt(D_ROWS * D_COLS / RANK)
    update = (factor * dot(unit_own * inverse, right_full, ((1,), (1,)))).astype(jnp.bfloat16)

    share = SHARD // CORE
    place = ((xh * ZH + lax.axis_index("zh")) * ZL + lax.axis_index("zl")) * SHARD + core * share
    own = lax.dynamic_slice_in_dim(right_full, place, share, 0) * inverse
    own = jnp.where(core == 0, own, jnp.concatenate([own[:, HALF:], own[:, :HALF]], axis=1))
    return (new_momentum, own[None], update)


def solution(mesh):
    fine = Mesh(
        mesh.devices.reshape(XH, ZH, ZL, CORE, 4, 2), ("xh", "zh", "zl", "core", "y", "xl")
    )
    block = P(ROW_AXES, COL_AXES)
    factor = P(COL_AXES, ROW_AXES, None)
    return jax.shard_map(
        on_device,
        mesh=fine,
        in_specs=(block, block, factor),
        out_specs=(block, factor, block),
        check_vma=False,
    )
```

```python
import math

import jax
import jax.numpy as jnp
from jax import lax
from jax.sharding import Mesh, PartitionSpec as P

D_ROWS = 12288
D_COLS = 12288
RANK = 512
HALF = RANK // 2

EPSILON = 1e-06
FEEDBACK = 0.1

XH, ZH, ZL, CORE = 2, 4, 4, 2
NZ = ZH * ZL
ROW_AXES = ("xh", "zh", "zl", "core")
COL_AXES = ("y", "xl")
Z_AXES = ("zh", "zl")
N_TP = 8
SHARD = 48
CLASS = ZH * SHARD
PAIR = [(0, 1), (1, 0)]
NEAR = ((0, 0), (0, 1), (0, 3), (1, 0))
CROSS = ((1, 1), (1, 3))
FAR = ((0, 2), (1, 2))


def dot(a, b, contract):
    return lax.dot_general(
        a, b, (contract, ((), ())), precision=lax.Precision.HIGH, preferred_element_type=jnp.float32
    )


def exchange(parts, axis):
    return lax.all_to_all(parts, axis, split_axis=0, concat_axis=0, tiled=True)


def spread(block, axis, count):
    return exchange(jnp.broadcast_to(block[None], (count,) + block.shape), axis)


def swap(block, axis):
    return lax.ppermute(block, axis, PAIR)


def step_z(block, by):
    return lax.ppermute(block, Z_AXES, [(z, (z + by) % NZ) for z in range(NZ)])


def step_two(block, sign):
    places = [(z, core) for z in range(NZ) for core in range(CORE)]
    moves = [(z * CORE + c, (z + (2 if c == 0 else -2) * sign) % NZ * CORE + c) for z, c in places]
    return lax.ppermute(block, Z_AXES + ("core",), moves)


def gather_near(shard):
    own = spread(shard, "zh", ZH).reshape(CLASS, HALF)
    after = step_z(own, -1)
    before = step_z(own, 1)
    beside = swap(own, "xh")
    return own, after, before, beside


def gather_rest(own, after, before, beside):
    cross = swap(jnp.concatenate([after, before]), "xh")
    far = step_two(jnp.concatenate([own, beside]), 1)
    return cross, far


def on_device(momentum, gradient, q_factor):
    xh = lax.axis_index("xh")
    zl = lax.axis_index("zl")
    core = lax.axis_index("core")
    blended = momentum + gradient.astype(jnp.float32)
    rows, cols = blended.shape

    own_q = q_factor[0].reshape(-1, CORE, HALF).transpose(1, 0, 2)
    chip_q = exchange(own_q, "core").reshape(SHARD, HALF)
    near = gather_near(chip_q)
    cross, far = gather_rest(*near)

    pair = jnp.concatenate([blended, swap(blended, "core")]).T.reshape(XH, ZH, ZL, SHARD, 2 * rows)

    def columns(pieces):
        picked = [
            lax.dynamic_slice(
                pair, (xh ^ e, 0, (zl + j) % ZL, 0, 0), (1, ZH, 1, SHARD, 2 * rows)
            ).reshape(CLASS, 2 * rows)
            for e, j in pieces
        ]
        return jnp.concatenate(picked)

    b_near, b_cross, b_far = columns(NEAR), columns(CROSS), columns(FAR)

    left_part = dot(b_near, jnp.concatenate(near), ((0,), (0,)))
    left_part = left_part + dot(b_cross, cross, ((0,), (0,))) + dot(b_far, far, ((0,), (0,)))
    by_tp = exchange(left_part.reshape(N_TP, SHARD, HALF), COL_AXES)
    left = spread(jnp.sum(by_tp, axis=0), COL_AXES, N_TP).reshape(2 * rows, HALF)

    squares = jnp.sum((left * left).reshape(-1, 8, HALF), axis=0)
    part_cross = dot(b_cross, left, ((1,), (0,)))
    part_far = dot(b_far, left, ((1,), (0,)))
    got_cross = swap(jnp.concatenate([part_cross, squares]), "xh")
    got_far = step_two(jnp.concatenate([part_far, squares]), -1)
    part = dot(b_near, left, ((1,), (0,)))
    squares_cross = squares + got_cross[2 * CLASS :]
    squares_far = squares + got_far[2 * CLASS :]
    to_after = jnp.concatenate([part[CLASS : 2 * CLASS] + got_cross[:CLASS], squares_cross])
    to_before = jnp.concatenate([part[2 * CLASS : 3 * CLASS] + got_cross[CLASS : 2 * CLASS], squares_cross])
    to_beside = jnp.concatenate([part[3 * CLASS :] + got_far[CLASS : 2 * CLASS], squares_far])
    own = jnp.concatenate([part[:CLASS] + got_far[:CLASS], squares_far])
    own = own + step_z(to_after, 1) + step_z(to_before, -1) + swap(to_beside, "xh")
    squares = own[CLASS:]
    own = own[:CLASS].reshape(ZH, SHARD, HALF)
    own = jnp.concatenate([own, jnp.broadcast_to(squares[None], (ZH,) + squares.shape)], axis=1)
    own = jnp.sum(exchange(own, "zh"), axis=0)
    left_norm = jnp.sqrt(jnp.sum(own[SHARD:], axis=0) + EPSILON)
    right = own[:SHARD] / left_norm
    left_unit = left / left_norm
    unit_own = jnp.concatenate([left_unit[:rows], swap(left_unit[rows:], "core")], axis=1)

    near = gather_near(right)
    cross, far = gather_rest(*near)
    own, after, before, beside = near
    mine = jnp.stack(
        [own, after, far[:CLASS], before, beside, cross[:CLASS], far[CLASS:], cross[CLASS:]]
    ).reshape(XH, ZL, ZH, SHARD, HALF)
    mine = jnp.where(xh == 0, mine, mine[::-1])
    mine = lax.dynamic_slice_in_dim(jnp.concatenate([mine, mine], axis=1), (ZL - zl) % ZL, ZL, 1)
    mine = mine.transpose(0, 2, 1, 3, 4).reshape(cols, HALF)
    right_full = jnp.concatenate([mine, swap(mine, "core")], axis=1)

    right_squares = jnp.sum((right_full * right_full).reshape(-1, 8, RANK), axis=0)
    right_squares = jnp.sum(spread(right_squares, COL_AXES, N_TP), axis=(0, 1))
    inverse = 1.0 / jnp.sqrt(right_squares + EPSILON)

    new_momentum = blended - FEEDBACK * dot(unit_own, right_full, ((1,), (1,)))
    factor = math.sqrt(D_ROWS * D_COLS / RANK)
    update = (factor * dot(unit_own * inverse, right_full, ((1,), (1,)))).astype(jnp.bfloat16)

    share = SHARD // CORE
    place = ((xh * ZH + lax.axis_index("zh")) * ZL + zl) * SHARD + core * share
    own_rows = lax.dynamic_slice_in_dim(right_full, place, share, 0) * inverse
    turned = jnp.concatenate([own_rows[:, HALF:], own_rows[:, :HALF]], axis=1)
    own_rows = jnp.where(core == 0, own_rows, turned)
    return (new_momentum, own_rows[None], update)


def solution(mesh):
    fine = Mesh(
        mesh.devices.reshape(XH, ZH, ZL, CORE, 4, 2), ("xh", "zh", "zl", "core", "y", "xl")
    )
    block = P(ROW_AXES, COL_AXES)
    factor = P(COL_AXES, ROW_AXES, None)
    return jax.shard_map(
        on_device,
        mesh=fine,
        in_specs=(block, block, factor),
        out_specs=(block, factor, block),
        check_vma=False,
    )
```

```python
import math

import jax
import jax.numpy as jnp
from jax import lax
from jax.sharding import Mesh, PartitionSpec as P

D_ROWS = 12288
D_COLS = 12288
RANK = 512

EPSILON = 1e-06
FEEDBACK = 0.1

XH, ZH, ZL, CORE = 2, 4, 4, 2
NZ = ZH * ZL
QUAD = XH * CORE
QUARTER = RANK // QUAD
ROW_AXES = ("xh", "zh", "zl", "core")
COL_AXES = ("y", "xl")
Z_AXES = ("zh", "zl")
N_TP = 8
SHARD = 48
ROWS_Z = XH * SHARD
CLASS = ZH * ROWS_Z
PAIR = [(0, 1), (1, 0)]


def dot(a, b, contract):
    return lax.dot_general(
        a, b, (contract, ((), ())), precision=lax.Precision.HIGH, preferred_element_type=jnp.float32
    )


def exchange(parts, axis):
    return lax.all_to_all(parts, axis, split_axis=0, concat_axis=0, tiled=True)


def spread(block, axis, count):
    return exchange(jnp.broadcast_to(block[None], (count,) + block.shape), axis)


def swap(block, axis):
    return lax.ppermute(block, axis, PAIR)


def step_z(block, by):
    return lax.ppermute(block, Z_AXES, [(z, (z + by) % NZ) for z in range(NZ)])


def step_two(block, sign):
    places = [(z, core) for z in range(NZ) for core in range(CORE)]
    moves = [(z * CORE + c, (z + (2 if c == 0 else -2) * sign) % NZ * CORE + c) for z, c in places]
    return lax.ppermute(block, Z_AXES + ("core",), moves)


def rolled(pieces, zl, width):
    stacked = jnp.stack(pieces + pieces).reshape(2 * ZL, ZH, XH, SHARD, width)
    natural = lax.dynamic_slice_in_dim(stacked, (ZL - zl) % ZL, ZL, 0)
    return natural.transpose(2, 1, 0, 3, 4).reshape(XH * NZ * SHARD, width)


def on_device(momentum, gradient, q_factor):
    xh = lax.axis_index("xh")
    zh = lax.axis_index("zh")
    zl = lax.axis_index("zl")
    core = lax.axis_index("core")
    blended = momentum + gradient.astype(jnp.float32)
    rows, cols = blended.shape

    beside = swap(blended, "xh")
    quad_rows = [blended, beside, swap(blended, "core"), swap(beside, "core")]

    own_q = q_factor[0].reshape(-1, QUAD, QUARTER).transpose(1, 0, 2)
    z_q = exchange(own_q, ("xh", "core")).reshape(ROWS_Z, QUARTER)
    own = spread(z_q, "zh", ZH).reshape(CLASS, QUARTER)
    after, before, far = step_z(own, -1), step_z(own, 1), step_two(own, 1)
    basis = rolled([own, after, far, before], zl, QUARTER)

    left_part = jnp.concatenate([dot(block, basis, ((1,), (0,))) for block in quad_rows])
    by_tp = exchange(left_part.reshape(N_TP, -1, QUARTER), COL_AXES)
    left = spread(jnp.sum(by_tp, axis=0), COL_AXES, N_TP).reshape(QUAD * rows, QUARTER)

    squares = jnp.sum((left * left).reshape(-1, 8, QUARTER), axis=0)
    lefts = left.reshape(QUAD, rows, QUARTER)
    part = sum(dot(quad_rows[i], lefts[i], ((0,), (0,))) for i in range(QUAD))
    part = part.reshape(XH, ZH, ZL, SHARD, QUARTER)

    def piece(j):
        block = lax.dynamic_slice_in_dim(part, (zl + j) % ZL, 1, 2)
        block = block.transpose(2, 1, 0, 3, 4).reshape(CLASS, QUARTER)
        return jnp.concatenate([block, squares])

    own = piece(0) + step_z(piece(1), 1) + step_z(piece(3), -1) + step_two(piece(2), -1)
    squares = own[CLASS:]
    own = own[:CLASS].reshape(ZH, ROWS_Z, QUARTER)
    own = jnp.concatenate([own, jnp.broadcast_to(squares[None], (ZH,) + squares.shape)], axis=1)
    own = exchange(own, "zh")

    left_x = swap(jnp.stack([lefts[1], lefts[3]]), "xh")
    left_c = swap(jnp.stack([lefts[2], left_x[1]]), "core")
    own, left_x, left_c = lax.optimization_barrier((own, left_x, left_c))
    left_own = jnp.concatenate([lefts[0], left_x[0], left_c[0], left_c[1]], axis=1)

    own = jnp.sum(own, axis=0)
    left_norm = jnp.sqrt(jnp.sum(own[ROWS_Z:], axis=0, keepdims=True) + EPSILON)
    right = own[:ROWS_Z] / left_norm
    norm_rows = jnp.broadcast_to(left_norm, (8, QUARTER))

    own = spread(right, "zh", ZH).reshape(CLASS, QUARTER)
    beside = swap(jnp.concatenate([own, norm_rows]), "xh")
    norm_rows = jnp.concatenate([norm_rows, beside[CLASS:]], axis=1)
    beside = beside[:CLASS]
    after, before = step_z(own, -1), step_z(own, 1)
    far = step_two(jnp.concatenate([own, beside]), 1)
    cross = swap(jnp.concatenate([after, before]), "xh")
    mine = rolled([own, after, far[:CLASS], before], zl, QUARTER)
    other = rolled([beside, cross[:CLASS], far[CLASS:], cross[CLASS:]], zl, QUARTER)
    both = jnp.concatenate([jnp.concatenate([mine, other], axis=1), norm_rows])
    both = jnp.concatenate([both, swap(both, "core")], axis=1)
    right_full = both[:cols]
    unit_own = left_own / both[cols : cols + 1]

    right_squares = jnp.sum((right_full * right_full).reshape(-1, 8, RANK), axis=0)
    right_squares = jnp.sum(spread(right_squares, COL_AXES, N_TP), axis=(0, 1))
    inverse = 1.0 / jnp.sqrt(right_squares + EPSILON)

    new_momentum = blended - FEEDBACK * dot(unit_own, right_full, ((1,), (1,)))
    factor = math.sqrt(D_ROWS * D_COLS / RANK)
    update = (factor * dot(unit_own * inverse, right_full, ((1,), (1,)))).astype(jnp.bfloat16)

    share = SHARD // CORE
    place = ((xh * ZH + zh) * ZL + zl) * SHARD + core * share
    own_rows = lax.dynamic_slice_in_dim(right_full, place, share, 0) * inverse
    own_rows = own_rows.reshape(share, CORE, XH, QUARTER)
    own_rows = jnp.where(core == 0, own_rows, own_rows[:, ::-1])
    own_rows = jnp.where(xh == 0, own_rows, own_rows[:, :, ::-1])
    own_rows = own_rows.transpose(0, 2, 1, 3).reshape(share, RANK)
    return (new_momentum, own_rows[None], update)


def solution(mesh):
    fine = Mesh(
        mesh.devices.reshape(XH, ZH, ZL, CORE, 4, 2), ("xh", "zh", "zl", "core", "y", "xl")
    )
    block = P(ROW_AXES, COL_AXES)
    factor = P(COL_AXES, ROW_AXES, None)
    return jax.shard_map(
        on_device,
        mesh=fine,
        in_specs=(block, block, factor),
        out_specs=(block, factor, block),
        check_vma=False,
    )
```

```python
import math

import jax
import jax.numpy as jnp
from jax import lax
from jax.sharding import Mesh, PartitionSpec as P

D_ROWS = 12288
D_COLS = 12288
RANK = 512

EPSILON = 1e-06
FEEDBACK = 0.1

XH, ZH, ZL, CORE = 2, 4, 4, 2
NZ = ZH * ZL
QUAD = XH * CORE
QUARTER = RANK // QUAD
ROW_AXES = ("xh", "zh", "zl", "core")
COL_AXES = ("y", "xl")
Z_AXES = ("zh", "zl")
N_TP = 8
SHARD = 48
ROWS_Z = XH * SHARD
CLASS = ZH * ROWS_Z
PAIR = [(0, 1), (1, 0)]


def dot(a, b, contract):
    return lax.dot_general(
        a, b, (contract, ((), ())), precision=lax.Precision.HIGH, preferred_element_type=jnp.float32
    )


def exchange(parts, axis):
    return lax.all_to_all(parts, axis, split_axis=0, concat_axis=0, tiled=True)


def spread(block, axis, count):
    return exchange(jnp.broadcast_to(block[None], (count,) + block.shape), axis)


def swap(block, axis):
    return lax.ppermute(block, axis, PAIR)


def step_z(block, by):
    return lax.ppermute(block, Z_AXES, [(z, (z + by) % NZ) for z in range(NZ)])


def step_two(block, sign):
    places = [(z, core) for z in range(NZ) for core in range(CORE)]
    moves = [(z * CORE + c, (z + (2 if c == 0 else -2) * sign) % NZ * CORE + c) for z, c in places]
    return lax.ppermute(block, Z_AXES + ("core",), moves)


def rolled(pieces, zl, width):
    stacked = jnp.stack(pieces + pieces).reshape(2 * ZL, ZH, XH, SHARD, width)
    natural = lax.dynamic_slice_in_dim(stacked, (ZL - zl) % ZL, ZL, 0)
    return natural.transpose(2, 1, 0, 3, 4).reshape(XH * NZ * SHARD, width)


def flipped(quarters, xh, core):
    quarters = jnp.where(xh == 0, quarters, quarters[:, ::-1])
    return jnp.where(core == 0, quarters, quarters[:, :, ::-1])


def on_device(momentum, gradient, q_factor):
    xh = lax.axis_index("xh")
    zh = lax.axis_index("zh")
    zl = lax.axis_index("zl")
    core = lax.axis_index("core")
    blended = momentum + gradient.astype(jnp.float32)
    rows, cols = blended.shape

    beside = swap(blended, "xh")
    across = swap(blended, "core")

    own_q = q_factor[0].reshape(-1, QUAD, QUARTER).transpose(1, 0, 2)
    z_q = exchange(own_q, ("xh", "core")).reshape(ROWS_Z, QUARTER)
    own = spread(z_q, "zh", ZH).reshape(CLASS, QUARTER)
    own, across = lax.optimization_barrier((own, across))
    quad_rows = [blended, beside, across, swap(beside, "core")]
    after, before, far = step_z(own, -1), step_z(own, 1), step_two(own, 1)
    basis = rolled([own, after, far, before], zl, QUARTER)

    left_part = jnp.concatenate([dot(block, basis, ((1,), (0,))) for block in quad_rows])
    by_tp = exchange(left_part.reshape(N_TP, -1, QUARTER), COL_AXES)
    left = spread(jnp.sum(by_tp, axis=0), COL_AXES, N_TP).reshape(QUAD * rows, QUARTER)

    squares = jnp.sum((left * left).reshape(-1, 8, QUARTER), axis=0)
    lefts = left.reshape(QUAD, rows, QUARTER)
    turned = [lax.optimization_barrier(block.T) for block in quad_rows]
    part = sum(dot(turned[i], lefts[i], ((1,), (0,))) for i in range(QUAD))
    part = part.reshape(XH, ZH, ZL, SHARD, QUARTER)

    def piece(j):
        block = lax.dynamic_slice_in_dim(part, (zl + j) % ZL, 1, 2)
        block = block.transpose(2, 1, 0, 3, 4).reshape(CLASS, QUARTER)
        return jnp.concatenate([block, squares])

    own = piece(0) + step_z(piece(1), 1) + step_z(piece(3), -1) + step_two(piece(2), -1)
    squares = own[CLASS:]
    own = own[:CLASS].reshape(ZH, ROWS_Z, QUARTER)
    own = jnp.concatenate([own, jnp.broadcast_to(squares[None], (ZH,) + squares.shape)], axis=1)
    own = exchange(own, "zh")
    own = jnp.sum(own, axis=0)
    left_norm = jnp.sqrt(jnp.sum(own[ROWS_Z:], axis=0, keepdims=True) + EPSILON)
    right = own[:ROWS_Z] / left_norm
    norm_rows = jnp.broadcast_to(left_norm, (8, QUARTER))

    own = spread(right, "zh", ZH).reshape(CLASS, QUARTER)
    payload = jnp.concatenate([own, norm_rows, lefts[1], lefts[3]])
    payload, own = lax.optimization_barrier((payload, own))
    beside = swap(payload, "xh")
    after, before, far = step_z(own, -1), step_z(own, 1), step_two(own, 1)
    cross = swap(jnp.concatenate([after, before, far]), "xh")

    squares = [jnp.sum((x * x).reshape(-1, 8, QUARTER), axis=0) for x in (own, after, before, far)]
    squares = spread(sum(squares), ("xh", "core") + COL_AXES, QUAD * N_TP)
    squares = jnp.sum(squares.reshape(XH, CORE, -1, QUARTER), axis=2)
    inverse = 1.0 / jnp.sqrt(squares + EPSILON)
    inverse = flipped(inverse[None], xh, core).reshape(RANK)

    mine = rolled([own, after, far, before], zl, QUARTER)
    mine = jnp.concatenate([mine, norm_rows, lefts[2]])
    mine_c = swap(mine, "core")
    cross, mine_c, inverse = lax.optimization_barrier((cross, mine_c, inverse))
    other = rolled(
        [beside[:CLASS], cross[:CLASS], cross[2 * CLASS :], cross[CLASS : 2 * CLASS]], zl, QUARTER
    )
    beside = beside[CLASS:]
    other = jnp.concatenate([other, beside[:8], beside[8 + rows :]])
    other_c = swap(other, "core")
    right_full = jnp.concatenate([x[:cols] for x in (mine, mine_c, other, other_c)], axis=1)
    norms = jnp.concatenate([x[cols : cols + 1] for x in (mine, mine_c, other, other_c)], axis=1)
    unit_own = [lefts[0], mine_c[cols + 8 :], beside[8 : 8 + rows], other_c[cols + 8 :]]
    unit_own = jnp.concatenate(unit_own, axis=1) / norms

    new_momentum = blended - FEEDBACK * dot(unit_own, right_full, ((1,), (1,)))
    factor = math.sqrt(D_ROWS * D_COLS / RANK)
    update = (factor * dot(unit_own * inverse, right_full, ((1,), (1,)))).astype(jnp.bfloat16)

    share = SHARD // CORE
    place = ((xh * ZH + zh) * ZL + zl) * SHARD + core * share
    own_rows = lax.dynamic_slice_in_dim(right_full, place, share, 0) * inverse
    own_rows = flipped(own_rows.reshape(share, XH, CORE, QUARTER), xh, core).reshape(share, RANK)
    return (new_momentum, own_rows[None], update)


def solution(mesh):
    fine = Mesh(
        mesh.devices.reshape(XH, ZH, ZL, CORE, 4, 2), ("xh", "zh", "zl", "core", "y", "xl")
    )
    block = P(ROW_AXES, COL_AXES)
    factor = P(COL_AXES, ROW_AXES, None)
    return jax.shard_map(
        on_device,
        mesh=fine,
        in_specs=(block, block, factor),
        out_specs=(block, factor, block),
        check_vma=False,
    )
```

```python
import math

import jax
import jax.numpy as jnp
from jax import lax
from jax.experimental import pallas as pl
from jax.experimental.pallas import tpu as pltpu
from jax.sharding import Mesh, PartitionSpec as P

D_ROWS = 12288
D_COLS = 12288
RANK = 512

EPSILON = 1e-06
FEEDBACK = 0.1

XH, ZH, ZL, CORE = 2, 4, 4, 2
NZ = ZH * ZL
QUAD = XH * CORE
QUARTER = RANK // QUAD
ROW_AXES = ("xh", "zh", "zl", "core")
COL_AXES = ("y", "xl")
Z_AXES = ("zh", "zl")
N_TP = 8
SHARD = 48
ROWS_Z = XH * SHARD
CLASS = ZH * ROWS_Z
PAIR = [(0, 1), (1, 0)]


def dot(a, b, contract):
    return lax.dot_general(
        a, b, (contract, ((), ())), precision=lax.Precision.HIGH, preferred_element_type=jnp.float32
    )


def exchange(parts, axis):
    return lax.all_to_all(parts, axis, split_axis=0, concat_axis=0, tiled=True)


def spread(block, axis, count):
    return exchange(jnp.broadcast_to(block[None], (count,) + block.shape), axis)


def swap(block, axis):
    return lax.ppermute(block, axis, PAIR)


def step_z(block, by):
    return lax.ppermute(block, Z_AXES, [(z, (z + by) % NZ) for z in range(NZ)])


def step_two(block, sign):
    places = [(z, core) for z in range(NZ) for core in range(CORE)]
    moves = [(z * CORE + c, (z + (2 if c == 0 else -2) * sign) % NZ * CORE + c) for z, c in places]
    return lax.ppermute(block, Z_AXES + ("core",), moves)


def rolled(pieces, zl, width):
    stacked = jnp.stack(pieces + pieces).reshape(2 * ZL, ZH, XH, SHARD, width)
    natural = lax.dynamic_slice_in_dim(stacked, (ZL - zl) % ZL, ZL, 0)
    return natural.transpose(2, 1, 0, 3, 4).reshape(XH * NZ * SHARD, width)


def halves(x):
    high = x.astype(jnp.bfloat16)
    return high, (x - high.astype(jnp.float32)).astype(jnp.bfloat16)


def finish_kernel(
    place, blended, left, packed, swapped, crossed, diagonal, squares,
    momentum_out, q_out, update_out, r_high, r_low, n_high, n_low, u_high, u_low,
):
    xh, zh, zl, core = place[0], place[1], place[2], place[3]
    rows = left.shape[0]

    @pl.when(pl.program_id(0) == 0)
    def _():
        quarters = (packed, swapped, crossed, diagonal)
        tail = ZL * CLASS
        units = ((left, 0), (swapped, tail + 8), (crossed, tail + 8), (diagonal, tail + 8 + rows))
        sums = [jnp.sum(squares[N_TP * 8 * q : N_TP * 8 * (q + 1), :], axis=0, keepdims=True) for q in range(QUAD)]
        inverse = turn([1.0 / jnp.sqrt(x + EPSILON) for x in sums], xh, core)
        q_rows = []
        for q in range(QUAD):
            lanes = pl.ds(q * QUARTER, QUARTER)
            ref = quarters[q]
            for j, offset in enumerate((0, 1, 3, 2)):
                base = j * CLASS
                at_class = lax.rem(zl + offset, ZL)
                for h in range(ZH):
                    for x in range(XH):
                        block = ref[base + h * ROWS_Z + x * SHARD : base + h * ROWS_Z + (x + 1) * SHARD, :]
                        start = pl.multiple_of((x * NZ + h * ZL + at_class) * SHARD, SHARD)
                        high, low = halves(block)
                        r_high[pl.ds(start, SHARD), lanes] = high
                        r_low[pl.ds(start, SHARD), lanes] = low
            unit_ref, base = units[q]
            unit = unit_ref[base : base + rows, :] / ref[tail : tail + 1, :]
            n_high[:, lanes], n_low[:, lanes] = halves(unit)
            u_high[:, lanes], u_low[:, lanes] = halves(unit * inverse[q])
            share = SHARD // CORE
            start = pl.multiple_of(zh * ROWS_Z + xh * SHARD + core * share, share)
            q_rows.append(ref[pl.ds(start, share), :] * inverse[q])
        for q, value in enumerate(turn(q_rows, xh, core)):
            q_out[:, q * QUARTER : (q + 1) * QUARTER] = value

    width = blended.shape[1]
    at = pl.ds(pl.multiple_of(pl.program_id(0) * width, width), width)
    high, low = r_high[at, :], r_low[at, :]

    def product(a_high, a_low):
        def one(a, b):
            return lax.dot_general(a, b, (((1,), (1,)), ((), ())), preferred_element_type=jnp.float32)

        return one(a_high[...], high) + (one(a_high[...], low) + one(a_low[...], high))

    momentum_out[...] = blended[...] - FEEDBACK * product(n_high, n_low)
    factor = math.sqrt(D_ROWS * D_COLS / RANK)
    update_out[...] = (factor * product(u_high, u_low)).astype(jnp.bfloat16)


def turn(quarters, xh, core):
    by_core = [jnp.where(core == 0, quarters[i], quarters[i ^ 1]) for i in range(QUAD)]
    return [jnp.where(xh == 0, by_core[i], by_core[i ^ 2]) for i in range(QUAD)]


def finish(place, blended, *whole):
    rows, cols = blended.shape
    width = 256
    block = pl.BlockSpec((rows, width), lambda i: (0, i))
    share = SHARD // CORE

    def full(x):
        return pl.BlockSpec(x.shape, lambda i: (0, 0))

    momentum, q_rows, update = pl.pallas_call(
        finish_kernel,
        grid=(cols // width,),
        in_specs=[pl.BlockSpec(memory_space=pltpu.SMEM), block] + [full(x) for x in whole],
        out_specs=[block, pl.BlockSpec((share, RANK), lambda i: (0, 0)), block],
        out_shape=[
            jax.ShapeDtypeStruct((rows, cols), jnp.float32),
            jax.ShapeDtypeStruct((share, RANK), jnp.float32),
            jax.ShapeDtypeStruct((rows, cols), jnp.bfloat16),
        ],
        scratch_shapes=[pltpu.VMEM((cols, RANK), jnp.bfloat16)] * 2
        + [pltpu.VMEM((rows, RANK), jnp.bfloat16)] * 4,
        compiler_params=pltpu.CompilerParams(vmem_limit_bytes=40 * 2**20),
        cost_estimate=pl.CostEstimate(flops=12 * rows * cols * RANK, bytes_accessed=10 * rows * cols, transcendentals=0),
        name="finish",
    )(place, blended, *whole)
    return momentum, q_rows[None], update


def on_device(momentum, gradient, q_factor):
    xh = lax.axis_index("xh")
    zh = lax.axis_index("zh")
    zl = lax.axis_index("zl")
    core = lax.axis_index("core")
    blended = momentum + gradient.astype(jnp.float32)
    rows, cols = blended.shape

    beside = swap(blended, "xh")
    quad_rows = [blended, beside, swap(blended, "core"), swap(beside, "core")]

    own_q = q_factor[0].reshape(-1, QUAD, QUARTER).transpose(1, 0, 2)
    z_q = exchange(own_q, ("xh", "core")).reshape(ROWS_Z, QUARTER)
    own = spread(z_q, "zh", ZH).reshape(CLASS, QUARTER)
    after, before, far = step_z(own, -1), step_z(own, 1), step_two(own, 1)
    basis = rolled([own, after, far, before], zl, QUARTER)

    left_part = jnp.concatenate([dot(block, basis, ((1,), (0,))) for block in quad_rows])
    by_tp = exchange(left_part.reshape(N_TP, -1, QUARTER), COL_AXES)
    left = spread(jnp.sum(by_tp, axis=0), COL_AXES, N_TP).reshape(QUAD * rows, QUARTER)

    squares = jnp.sum((left * left).reshape(-1, 8, QUARTER), axis=0)
    lefts = left.reshape(QUAD, rows, QUARTER)
    part = sum(dot(quad_rows[i], lefts[i], ((0,), (0,))) for i in range(QUAD))
    part = part.reshape(XH, ZH, ZL, SHARD, QUARTER)

    def piece(j):
        block = lax.dynamic_slice_in_dim(part, (zl + j) % ZL, 1, 2)
        block = block.transpose(2, 1, 0, 3, 4).reshape(CLASS, QUARTER)
        return jnp.concatenate([block, squares])

    own = piece(0) + step_z(piece(1), 1) + step_z(piece(3), -1) + step_two(piece(2), -1)
    squares = own[CLASS:]
    own = own[:CLASS].reshape(ZH, ROWS_Z, QUARTER)
    own = jnp.concatenate([own, jnp.broadcast_to(squares[None], (ZH,) + squares.shape)], axis=1)
    own = exchange(own, "zh")
    own = jnp.sum(own, axis=0)
    left_norm = jnp.sqrt(jnp.sum(own[ROWS_Z:], axis=0, keepdims=True) + EPSILON)
    right = own[:ROWS_Z] / left_norm
    norm_rows = jnp.broadcast_to(left_norm, (8, QUARTER))

    own = spread(right, "zh", ZH).reshape(CLASS, QUARTER)
    after, before, far = step_z(own, -1), step_z(own, 1), step_two(own, 1)
    near = [own, after, before, far, norm_rows]
    packed = jnp.concatenate(near + [lefts[1], lefts[3]])
    packed, near = lax.optimization_barrier((packed, near))
    crossed = swap(packed, "xh")
    swapped = swap(jnp.concatenate(near + [lefts[2]]), "core")
    squares = sum(jnp.sum((x * x).reshape(-1, 8, QUARTER), axis=0) for x in near[:ZL])
    squares = spread(squares, ("xh", "core") + COL_AXES, QUAD * N_TP).reshape(-1, QUARTER)
    crossed, swapped, squares = lax.optimization_barrier((crossed, swapped, squares))
    diagonal = swap(crossed, "core")

    place = jnp.stack([xh, zh, zl, core]).astype(jnp.int32)
    return finish(place, blended, lefts[0], packed, swapped, crossed, diagonal, squares)


def solution(mesh):
    fine = Mesh(
        mesh.devices.reshape(XH, ZH, ZL, CORE, 4, 2), ("xh", "zh", "zl", "core", "y", "xl")
    )
    block = P(ROW_AXES, COL_AXES)
    factor = P(COL_AXES, ROW_AXES, None)
    return jax.shard_map(
        on_device,
        mesh=fine,
        in_specs=(block, block, factor),
        out_specs=(block, factor, block),
        check_vma=False,
    )
```

```python
import math

import jax
import jax.numpy as jnp
from jax import lax
from jax.experimental import pallas as pl
from jax.experimental.layout import Layout, with_layout_constraint
from jax.experimental.pallas import tpu as pltpu
from jax.sharding import Mesh, PartitionSpec as P

D_ROWS = 12288
D_COLS = 12288
RANK = 512

EPSILON = 1e-06
FEEDBACK = 0.1

XH, ZH, ZL, CORE = 2, 4, 4, 2
NZ = ZH * ZL
QUAD = XH * CORE
QUARTER = RANK // QUAD
ROW_AXES = ("xh", "zh", "zl", "core")
COL_AXES = ("y", "xl")
Z_AXES = ("zh", "zl")
N_TP = 8
SHARD = 48
ROWS_Z = XH * SHARD
CLASS = ZH * ROWS_Z
PAIR = [(0, 1), (1, 0)]


def dot(a, b, contract):
    return lax.dot_general(
        a, b, (contract, ((), ())), precision=lax.Precision.HIGH, preferred_element_type=jnp.float32
    )


def exchange(parts, axis):
    return lax.all_to_all(parts, axis, split_axis=0, concat_axis=0, tiled=True)


def spread(block, axis, count):
    return exchange(jnp.broadcast_to(block[None], (count,) + block.shape), axis)


def swap(block, axis):
    return lax.ppermute(block, axis, PAIR)


def step_z(block, by):
    return lax.ppermute(block, Z_AXES, [(z, (z + by) % NZ) for z in range(NZ)])


def step_two(block, sign):
    places = [(z, core) for z in range(NZ) for core in range(CORE)]
    moves = [(z * CORE + c, (z + (2 if c == 0 else -2) * sign) % NZ * CORE + c) for z, c in places]
    return lax.ppermute(block, Z_AXES + ("core",), moves)


def rolled(pieces, zl, width):
    stacked = jnp.stack(pieces + pieces).reshape(2 * ZL, ZH, XH, SHARD, width)
    natural = lax.dynamic_slice_in_dim(stacked, (ZL - zl) % ZL, ZL, 0)
    return natural.transpose(2, 1, 0, 3, 4).reshape(XH * NZ * SHARD, width)


def halves(x):
    high = x.astype(jnp.bfloat16)
    return high, (x - high.astype(jnp.float32)).astype(jnp.bfloat16)


def finish_kernel(
    place, blended, left, packed, swapped, crossed, diagonal, squares,
    momentum_out, q_out, update_out, r_high, r_low, n_high, n_low, u_high, u_low,
):
    xh, zh, zl, core = place[0], place[1], place[2], place[3]
    rows = left.shape[0]

    @pl.when(pl.program_id(0) == 0)
    def _():
        quarters = (packed, swapped, crossed, diagonal)
        tail = ZL * CLASS
        units = ((left, 0), (swapped, tail + 8), (crossed, tail + 8), (diagonal, tail + 8 + rows))
        sums = [jnp.sum(squares[N_TP * 8 * q : N_TP * 8 * (q + 1), :], axis=0, keepdims=True) for q in range(QUAD)]
        inverse = turn([1.0 / jnp.sqrt(x + EPSILON) for x in sums], xh, core)
        q_rows = []
        for q in range(QUAD):
            lanes = pl.ds(q * QUARTER, QUARTER)
            ref = quarters[q]
            for j, offset in enumerate((0, 1, 3, 2)):
                base = j * CLASS
                at_class = lax.rem(zl + offset, ZL)
                for h in range(ZH):
                    for x in range(XH):
                        block = ref[base + h * ROWS_Z + x * SHARD : base + h * ROWS_Z + (x + 1) * SHARD, :]
                        start = pl.multiple_of((x * NZ + h * ZL + at_class) * SHARD, SHARD)
                        high, low = halves(block)
                        r_high[pl.ds(start, SHARD), lanes] = high
                        r_low[pl.ds(start, SHARD), lanes] = low
            unit_ref, base = units[q]
            unit = unit_ref[base : base + rows, :] / ref[tail : tail + 1, :]
            n_high[:, lanes], n_low[:, lanes] = halves(unit)
            u_high[:, lanes], u_low[:, lanes] = halves(unit * inverse[q])
            share = SHARD // CORE
            start = pl.multiple_of(zh * ROWS_Z + xh * SHARD + core * share, share)
            q_rows.append(ref[pl.ds(start, share), :] * inverse[q])
        for q, value in enumerate(turn(q_rows, xh, core)):
            q_out[:, q * QUARTER : (q + 1) * QUARTER] = value

    width = blended.shape[1]
    at = pl.ds(pl.multiple_of(pl.program_id(0) * width, width), width)
    high, low = r_high[at, :], r_low[at, :]

    def product(a_high, a_low):
        def one(a, b):
            return lax.dot_general(a, b, (((1,), (1,)), ((), ())), preferred_element_type=jnp.float32)

        return one(a_high[...], high) + (one(a_high[...], low) + one(a_low[...], high))

    momentum_out[...] = blended[...] - FEEDBACK * product(n_high, n_low)
    factor = math.sqrt(D_ROWS * D_COLS / RANK)
    update_out[...] = (factor * product(u_high, u_low)).astype(jnp.bfloat16)


def turn(quarters, xh, core):
    by_core = [jnp.where(core == 0, quarters[i], quarters[i ^ 1]) for i in range(QUAD)]
    return [jnp.where(xh == 0, by_core[i], by_core[i ^ 2]) for i in range(QUAD)]


def finish(place, blended, *whole):
    rows, cols = blended.shape
    width = 256
    block = pl.BlockSpec((rows, width), lambda i: (0, i))
    share = SHARD // CORE

    momentum, q_rows, update = pl.pallas_call(
        finish_kernel,
        grid=(cols // width,),
        in_specs=[pl.BlockSpec(memory_space=pltpu.SMEM), block] + [pl.BlockSpec(memory_space=pltpu.VMEM)] * len(whole),
        out_specs=[block, pl.BlockSpec((share, RANK), lambda i: (0, 0)), block],
        out_shape=[
            jax.ShapeDtypeStruct((rows, cols), jnp.float32),
            jax.ShapeDtypeStruct((share, RANK), jnp.float32),
            jax.ShapeDtypeStruct((rows, cols), jnp.bfloat16),
        ],
        scratch_shapes=[pltpu.VMEM((cols, RANK), jnp.bfloat16)] * 2
        + [pltpu.VMEM((rows, RANK), jnp.bfloat16)] * 4,
        compiler_params=pltpu.CompilerParams(vmem_limit_bytes=24 * 2**20),
        cost_estimate=pl.CostEstimate(flops=12 * rows * cols * RANK, bytes_accessed=10 * rows * cols, transcendentals=0),
        name="finish",
    )(place, blended, *whole)
    return momentum, q_rows[None], update


def on_device(momentum, gradient, q_factor):
    xh = lax.axis_index("xh")
    zh = lax.axis_index("zh")
    zl = lax.axis_index("zl")
    core = lax.axis_index("core")
    blended = momentum + gradient.astype(jnp.float32)
    rows, cols = blended.shape

    beside = swap(blended, "xh")
    quad_rows = [blended, beside, swap(blended, "core"), swap(beside, "core")]

    own_q = q_factor[0].reshape(-1, QUAD, QUARTER).transpose(1, 0, 2)
    z_q = exchange(own_q, ("xh", "core")).reshape(ROWS_Z, QUARTER)
    own = spread(z_q, "zh", ZH).reshape(CLASS, QUARTER)
    after, before, far = step_z(own, -1), step_z(own, 1), step_two(own, 1)
    basis = rolled([own, after, far, before], zl, QUARTER)

    left_part = jnp.concatenate([dot(block, basis, ((1,), (0,))) for block in quad_rows])
    by_tp = exchange(left_part.reshape(N_TP, -1, QUARTER), COL_AXES)
    left = spread(jnp.sum(by_tp, axis=0), COL_AXES, N_TP).reshape(QUAD * rows, QUARTER)

    squares = jnp.sum((left * left).reshape(-1, 8, QUARTER), axis=0)
    lefts = left.reshape(QUAD, rows, QUARTER)
    turned = sum(dot(lefts[i], quad_rows[i], ((0,), (0,))) for i in range(QUAD))
    part = with_layout_constraint(turned, Layout(major_to_minor=(0, 1))).T
    part = part.reshape(XH, ZH, ZL, SHARD, QUARTER)

    def piece(j):
        block = lax.dynamic_slice_in_dim(part, (zl + j) % ZL, 1, 2)
        block = block.transpose(2, 1, 0, 3, 4).reshape(CLASS, QUARTER)
        return jnp.concatenate([block, squares])

    own = piece(0) + step_z(piece(1), 1) + step_z(piece(3), -1) + step_two(piece(2), -1)
    squares = own[CLASS:]
    own = own[:CLASS].reshape(ZH, ROWS_Z, QUARTER)
    own = jnp.concatenate([own, jnp.broadcast_to(squares[None], (ZH,) + squares.shape)], axis=1)
    own = exchange(own, "zh")
    own = jnp.sum(own, axis=0)
    left_norm = jnp.sqrt(jnp.sum(own[ROWS_Z:], axis=0, keepdims=True) + EPSILON)
    right = own[:ROWS_Z] / left_norm
    norm_rows = jnp.broadcast_to(left_norm, (8, QUARTER))

    own = spread(right, "zh", ZH).reshape(CLASS, QUARTER)
    after, before, far = step_z(own, -1), step_z(own, 1), step_two(own, 1)
    near = [own, after, before, far, norm_rows]
    packed = jnp.concatenate(near + [lefts[1], lefts[3]])
    packed, near = lax.optimization_barrier((packed, near))
    crossed = swap(packed, "xh")
    swapped = swap(jnp.concatenate(near + [lefts[2]]), "core")
    squares = sum(jnp.sum((x * x).reshape(-1, 8, QUARTER), axis=0) for x in near[:ZL])
    squares = spread(squares, ("xh", "core") + COL_AXES, QUAD * N_TP).reshape(-1, QUARTER)
    crossed, swapped, squares = lax.optimization_barrier((crossed, swapped, squares))
    diagonal = swap(crossed, "core")

    place = jnp.stack([xh, zh, zl, core]).astype(jnp.int32)
    return finish(place, blended, lefts[0], packed, swapped, crossed, diagonal, squares)


def solution(mesh):
    fine = Mesh(
        mesh.devices.reshape(XH, ZH, ZL, CORE, 4, 2), ("xh", "zh", "zl", "core", "y", "xl")
    )
    block = P(ROW_AXES, COL_AXES)
    factor = P(COL_AXES, ROW_AXES, None)
    return jax.shard_map(
        on_device,
        mesh=fine,
        in_specs=(block, block, factor),
        out_specs=(block, factor, block),
        check_vma=False,
    )
```

```python
import math

import jax
import jax.numpy as jnp
from jax import lax
from jax.experimental import pallas as pl
from jax.experimental.layout import Layout, with_layout_constraint
from jax.experimental.pallas import tpu as pltpu
from jax.sharding import Mesh, PartitionSpec as P

D_ROWS = 12288
D_COLS = 12288
RANK = 512

EPSILON = 1e-06
FEEDBACK = 0.1

XH, ZH, ZL, CORE = 2, 4, 4, 2
NZ = ZH * ZL
QUAD = XH * CORE
QUARTER = RANK // QUAD
ROW_AXES = ("xh", "zh", "zl", "core")
COL_AXES = ("y", "xl")
Z_AXES = ("zh", "zl")
N_TP = 8
SHARD = 48
ROWS_Z = XH * SHARD
CLASS = ZH * ROWS_Z
PAIR = [(0, 1), (1, 0)]


def dot(a, b, contract):
    return lax.dot_general(
        a, b, (contract, ((), ())), precision=lax.Precision.HIGH, preferred_element_type=jnp.float32
    )


def exchange(parts, axis):
    return lax.all_to_all(parts, axis, split_axis=0, concat_axis=0, tiled=True)


def spread(block, axis, count):
    return exchange(jnp.broadcast_to(block[None], (count,) + block.shape), axis)


def swap(block, axis):
    return lax.ppermute(block, axis, PAIR)


def step_z(block, by):
    return lax.ppermute(block, Z_AXES, [(z, (z + by) % NZ) for z in range(NZ)])


def step_two(block, sign):
    places = [(z, core) for z in range(NZ) for core in range(CORE)]
    moves = [(z * CORE + c, (z + (2 if c == 0 else -2) * sign) % NZ * CORE + c) for z, c in places]
    return lax.ppermute(block, Z_AXES + ("core",), moves)


def rolled(pieces, zl, width):
    stacked = jnp.stack(pieces + pieces).reshape(2 * ZL, ZH, XH, SHARD, width)
    natural = lax.dynamic_slice_in_dim(stacked, (ZL - zl) % ZL, ZL, 0)
    return natural.transpose(2, 1, 0, 3, 4).reshape(XH * NZ * SHARD, width)


def halves(x):
    high = x.astype(jnp.bfloat16)
    return high, (x - high.astype(jnp.float32)).astype(jnp.bfloat16)


def finish_kernel(
    place, blended, left, left_x, packed, swapped, crossed, diagonal, squares,
    momentum_out, q_out, update_out, r_high, r_low, n_high, n_low, u_high, u_low,
):
    xh, zh, zl, core = place[0], place[1], place[2], place[3]
    rows = left.shape[0]

    @pl.when(pl.program_id(0) == 0)
    def _():
        quarters = (packed, swapped, crossed, diagonal)
        tail = ZL * CLASS
        units = ((left, 0), (swapped, tail + 8), (left_x, 0), (swapped, tail + 8 + rows))
        sums = [jnp.sum(squares[N_TP * 8 * q : N_TP * 8 * (q + 1), :], axis=0, keepdims=True) for q in range(QUAD)]
        inverse = turn([1.0 / jnp.sqrt(x + EPSILON) for x in sums], xh, core)
        q_rows = []
        for q in range(QUAD):
            lanes = pl.ds(q * QUARTER, QUARTER)
            ref = quarters[q]
            for j, offset in enumerate((0, 1, 3, 2)):
                base = j * CLASS
                at_class = lax.rem(zl + offset, ZL)
                for h in range(ZH):
                    for x in range(XH):
                        block = ref[base + h * ROWS_Z + x * SHARD : base + h * ROWS_Z + (x + 1) * SHARD, :]
                        start = pl.multiple_of((x * NZ + h * ZL + at_class) * SHARD, SHARD)
                        high, low = halves(block)
                        r_high[pl.ds(start, SHARD), lanes] = high
                        r_low[pl.ds(start, SHARD), lanes] = low
            unit_ref, base = units[q]
            unit = unit_ref[base : base + rows, :] / ref[tail : tail + 1, :]
            n_high[:, lanes], n_low[:, lanes] = halves(unit)
            u_high[:, lanes], u_low[:, lanes] = halves(unit * inverse[q])
            share = SHARD // CORE
            start = pl.multiple_of(zh * ROWS_Z + xh * SHARD + core * share, share)
            q_rows.append(ref[pl.ds(start, share), :] * inverse[q])
        for q, value in enumerate(turn(q_rows, xh, core)):
            q_out[:, q * QUARTER : (q + 1) * QUARTER] = value

    width = blended.shape[1]
    at = pl.ds(pl.multiple_of(pl.program_id(0) * width, width), width)
    high, low = r_high[at, :], r_low[at, :]

    def product(a_high, a_low):
        def one(a, b):
            return lax.dot_general(a, b, (((1,), (1,)), ((), ())), preferred_element_type=jnp.float32)

        return one(a_high[...], high) + (one(a_high[...], low) + one(a_low[...], high))

    momentum_out[...] = blended[...] - FEEDBACK * product(n_high, n_low)
    factor = math.sqrt(D_ROWS * D_COLS / RANK)
    update_out[...] = (factor * product(u_high, u_low)).astype(jnp.bfloat16)


def turn(quarters, xh, core):
    by_core = [jnp.where(core == 0, quarters[i], quarters[i ^ 1]) for i in range(QUAD)]
    return [jnp.where(xh == 0, by_core[i], by_core[i ^ 2]) for i in range(QUAD)]


def finish(place, blended, *whole):
    rows, cols = blended.shape
    width = 256
    block = pl.BlockSpec((rows, width), lambda i: (0, i))
    share = SHARD // CORE

    momentum, q_rows, update = pl.pallas_call(
        finish_kernel,
        grid=(cols // width,),
        in_specs=[pl.BlockSpec(memory_space=pltpu.SMEM), block] + [pl.BlockSpec(memory_space=pltpu.VMEM)] * len(whole),
        out_specs=[block, pl.BlockSpec((share, RANK), lambda i: (0, 0)), block],
        out_shape=[
            jax.ShapeDtypeStruct((rows, cols), jnp.float32),
            jax.ShapeDtypeStruct((share, RANK), jnp.float32),
            jax.ShapeDtypeStruct((rows, cols), jnp.bfloat16),
        ],
        scratch_shapes=[pltpu.VMEM((cols, RANK), jnp.bfloat16)] * 2
        + [pltpu.VMEM((rows, RANK), jnp.bfloat16)] * 4,
        compiler_params=pltpu.CompilerParams(vmem_limit_bytes=12 * 2**20),
        cost_estimate=pl.CostEstimate(flops=12 * rows * cols * RANK, bytes_accessed=10 * rows * cols, transcendentals=0),
        name="finish",
    )(place, blended, *whole)
    return momentum, q_rows[None], update


def on_device(momentum, gradient, q_factor):
    xh = lax.axis_index("xh")
    zh = lax.axis_index("zh")
    zl = lax.axis_index("zl")
    core = lax.axis_index("core")
    blended = momentum + gradient.astype(jnp.float32)
    rows, cols = blended.shape

    beside = swap(blended, "xh")
    quad_rows = [blended, beside, swap(blended, "core"), swap(beside, "core")]

    own_q = q_factor[0].reshape(-1, QUAD, QUARTER).transpose(1, 0, 2)
    z_q = exchange(own_q, ("xh", "core")).reshape(ROWS_Z, QUARTER)
    own = spread(z_q, "zh", ZH).reshape(CLASS, QUARTER)
    after, before, far = step_z(own, -1), step_z(own, 1), step_two(own, 1)
    basis = rolled([own, after, far, before], zl, QUARTER)

    left_part = jnp.concatenate([dot(block, basis, ((1,), (0,))) for block in quad_rows])
    by_tp = exchange(left_part.reshape(N_TP, -1, QUARTER), COL_AXES)
    left = spread(jnp.sum(by_tp, axis=0), COL_AXES, N_TP).reshape(QUAD * rows, QUARTER)

    squares = jnp.sum((left * left).reshape(-1, 8, QUARTER), axis=0)
    lefts = left.reshape(QUAD, rows, QUARTER)
    turned = sum(dot(lefts[i], quad_rows[i], ((0,), (0,))) for i in range(QUAD))
    part = with_layout_constraint(turned, Layout(major_to_minor=(0, 1))).T
    part = with_layout_constraint(part, Layout(major_to_minor=(1, 0)))
    part = part.reshape(XH, ZH, ZL, SHARD, QUARTER)

    def piece(j):
        block = lax.dynamic_slice_in_dim(part, (zl + j) % ZL, 1, 2)
        block = block.transpose(2, 1, 0, 3, 4).reshape(CLASS, QUARTER)
        return jnp.concatenate([block, squares])

    moved = step_z(piece(1), 1), step_z(piece(3), -1), step_two(piece(2), -1)
    left_x = swap(jnp.concatenate([lefts[1], lefts[3]]), "xh")
    moved, left_x = lax.optimization_barrier((moved, left_x))
    own = piece(0) + sum(moved)
    squares = own[CLASS:]
    own = own[:CLASS].reshape(ZH, ROWS_Z, QUARTER)
    own = jnp.concatenate([own, jnp.broadcast_to(squares[None], (ZH,) + squares.shape)], axis=1)
    own = exchange(own, "zh")
    own = jnp.sum(own, axis=0)
    left_norm = jnp.sqrt(jnp.sum(own[ROWS_Z:], axis=0, keepdims=True) + EPSILON)
    right = own[:ROWS_Z] / left_norm
    norm_rows = jnp.broadcast_to(left_norm, (8, QUARTER))

    own = spread(right, "zh", ZH).reshape(CLASS, QUARTER)
    after, before, far = step_z(own, -1), step_z(own, 1), step_two(own, 1)
    near = [own, after, before, far, norm_rows]
    packed = jnp.concatenate(near)
    packed, near = lax.optimization_barrier((packed, near))
    crossed = swap(packed, "xh")
    swapped = swap(jnp.concatenate(near + [lefts[2], left_x[rows:]]), "core")
    squares = sum(jnp.sum((x * x).reshape(-1, 8, QUARTER), axis=0) for x in near[:ZL])
    squares = spread(squares, ("xh", "core") + COL_AXES, QUAD * N_TP).reshape(-1, QUARTER)
    crossed, swapped, squares = lax.optimization_barrier((crossed, swapped, squares))
    diagonal = swap(crossed, "core")

    place = jnp.stack([xh, zh, zl, core]).astype(jnp.int32)
    return finish(place, blended, lefts[0], left_x, packed, swapped, crossed, diagonal, squares)


def solution(mesh):
    fine = Mesh(
        mesh.devices.reshape(XH, ZH, ZL, CORE, 4, 2), ("xh", "zh", "zl", "core", "y", "xl")
    )
    block = P(ROW_AXES, COL_AXES)
    factor = P(COL_AXES, ROW_AXES, None)
    return jax.shard_map(
        on_device,
        mesh=fine,
        in_specs=(block, block, factor),
        out_specs=(block, factor, block),
        check_vma=False,
    )
```
